32 devices in a mesh: row: 16 (over z, y, core), col: 2 (over x).
Axes of the slice: x: 2, y: 2, z: 4, core: 2. Of those that a mesh axis runs over, the one named last changes fastest.
Arguments:
- trailing_adj: bfloat16 [8, 16, 256, 64, 2, 256], P(None, 'row', None, None, 'col'), may hold values from -6 to 6
- factor_panel: bfloat16 [8, 16, 256, 256], P(None, 'row', 'col'), may hold values from -0.03125 to 0.03125
- panel_adj: float32 [8, 16, 256, 256], P(None, 'row', 'col'), may hold values from -6 to 6
- inverse_diag: float32 [256, 256], replicated, may hold values from -1 to 2, as said below
- diag_adjoint: float32 [256, 256], replicated, may hold values from -6 to 6
Outputs:
- panel_grad: float32 [8, 16, 256, 256], P(None, 'row', 'col')
- diag_grad: float32 [256, 256], replicated
The draws below stay inside these ranges and needn't reach their ends.
Inputs may be any that keep to these rules, and one draw needn't show every extreme that they name: inverse_diag is lower triangular, with diagonal entries between 0.75 and 1.25.
All inputs are finite; a program needn't handle non-finite values.
Results may differ from the reference program's by a relative error of at most 0.0003.
Values may be sent and summed in bfloat16 or wider, within the bound.
No kernel may reach another device: no remote copies, remote signals or barrier semaphores. Data moves between devices by JAX's collectives and lax.ppermute only.
A program may use at most 320 MiB of HBM per device.

```python
import jax
import jax.numpy as jnp
from jax import lax

ORDER = 32768
WIDTH = 256
ROW_BLOCKS = 8
COL_BLOCKS = 64
N_ROW = 16
N_COL = 2


def draw_inverse_diag(key, part):
    key = jax.random.fold_in(key, 7)
    values = jax.random.truncated_normal(key, -4.0, 4.0, (WIDTH, WIDTH), jnp.float32)
    return jnp.tril(values) / WIDTH ** 0.5 + jnp.eye(WIDTH, dtype=jnp.float32)


def block_scale(key, shape, shards, low, high):
    gain = 1.0
    for position, parts in shards:
        steps = jax.random.uniform(jax.random.fold_in(jax.random.fold_in(key, 6), position), (parts,), jnp.float32, low / len(shards), high / len(shards))
        gain = gain * jnp.repeat(jnp.exp(steps), shape[position] // parts).reshape((-1,) + (1,) * (len(shape) - 1 - position))
    return gain


def gaussian(own_key, shape, spread, reach, shards=(), held_as=jnp.bfloat16):
    values = spread * jax.random.normal(own_key, shape, jnp.float32)
    if shards:
        values = values * block_scale(own_key, shape, shards, -0.22, 0.18)
    return jnp.clip(values, -reach, reach).astype(held_as)


def setup_inputs(seed: int = 0) -> dict:
    key_list = jax.random.split(jax.random.key(seed), 6)
    return {
        "trailing_adj": gaussian(key_list[0], (ROW_BLOCKS, N_ROW, WIDTH, COL_BLOCKS, N_COL, WIDTH), 1.0, 6.0, ((1, 16), (4, 2))),
        "factor_panel": gaussian(key_list[1], (ROW_BLOCKS, N_ROW, WIDTH, WIDTH), ORDER ** -0.5, 0.03125, ((1, 16), (2, 2))),
        "panel_adj": gaussian(key_list[2], (ROW_BLOCKS, N_ROW, WIDTH, WIDTH), 1.0, 6.0, ((1, 16), (2, 2)), jnp.float32),
        "inverse_diag": draw_inverse_diag(jax.random.fold_in(key_list[5], 71), 0),
        "diag_adjoint": gaussian(key_list[4], (WIDTH, WIDTH), 1.0, 6.0, (), jnp.float32),
    }


def reference(trailing_adj, factor_panel, panel_adj, inverse_diag, diag_adjoint):
    matrix = trailing_adj.reshape(ORDER, ORDER)
    lower_panel = factor_panel.reshape(ORDER, WIDTH)
    forward = jnp.dot(matrix, lower_panel, preferred_element_type=jnp.float32)
    backward = lax.dot_general(matrix, lower_panel, (((0,), (0,)), ((), ())), preferred_element_type=jnp.float32)
    combined = panel_adj.reshape(ORDER, WIDTH) - forward - backward
    panel_grad = jnp.dot(combined, inverse_diag, precision=lax.Precision.HIGHEST)
    cross = lax.dot_general(lower_panel.astype(jnp.float32), combined, (((0,), (0,)), ((), ())), precision=lax.Precision.HIGHEST)
    diag_grad = diag_adjoint - jnp.dot(inverse_diag.T, cross.T, precision=lax.Precision.HIGHEST)
    return panel_grad.reshape(ROW_BLOCKS, N_ROW, WIDTH, WIDTH), diag_grad
```

```python
import functools
import math

import jax
import jax.numpy as jnp
from jax import lax
from jax.experimental import pallas as pl
from jax.experimental.pallas import tpu as pltpu
from jax.sharding import PartitionSpec as P

F32, F16, BF16 = jnp.float32, jnp.float16, jnp.bfloat16
STEP_ROWS = 1024
GROUP = 16
VMEM = 52 << 20
COST = 4


def bits(low, high):
    return [1 << i for i in range(low.bit_length() - 1, high.bit_length() - 1)]


def place(mask, weights):
    return sum(w for i, w in enumerate(weights) if (mask >> i) & 1)


def panel_kernel(back, fwd, nk, nq, count, first, weights, *refs):
    refs = list(refs)
    take = lambda n: [refs.pop(0) for _ in range(n)]
    (pos_ref, s_ref) = take(2)
    (lr_ref,) = take(1) if back else (None,)
    l_refs = take(nk) if fwd else []
    (f_in,) = take(1) if fwd and not first else (None,)
    take(count)
    b_refs = take(nk) if back else []
    (f_ref,) = take(1) if fwd else (None,)
    (zero_ref,) = take(1)
    (acc,) = take(1) if back else (None,)
    (col,) = take(1) if fwd else (None,)
    i, last = pl.program_id(0), pl.num_programs(0) - 1
    _, group, width = s_ref.shape
    piece = width // nk

    def places():
        for dk in range(nk):
            at = pl.multiple_of(jnp.bitwise_xor(pos_ref[0], dk) * piece, piece)
            for m in range(nq):
                q = jnp.bitwise_xor(pos_ref[1], m)
                for kk in range(group // nq):
                    yield dk, place(m, weights), kk, kk * nq + q, at

    @pl.when(i == 0)
    def _():
        zero_ref[0, 0] = 0.0

    x = jnp.swapaxes(s_ref[...], 0, 1)
    if fwd:

        @pl.when(i == 0)
        def _():
            for dk, m, kk, j, at in places():
                col[j, pl.ds(at, piece), :] = l_refs[dk][m, kk]

        flat = jnp.concatenate([x[j] for j in range(group)], axis=1)
        part = jnp.dot(flat, col[...].reshape(group * width, -1), preferred_element_type=F32)
        f_ref[...] = part if first else f_in[...] + part
    if back:

        def product(j):
            return lax.dot_general(
                x[j], lr_ref[...], (((0,), (0,)), ((), ())), preferred_element_type=F32
            )

        @pl.when(i == 0)
        def _():
            for j in range(group):
                acc[j] = product(j)

        @pl.when(i > 0)
        def _():
            for j in range(group):
                acc[j] += product(j)

        @pl.when(i == last)
        def _():
            for dk, m, kk, j, at in places():
                b_refs[dk][m, kk] = acc[j, pl.ds(at, piece), :]


def panel_call(back, fwd, chunk, nk, nq, weights, pos, s, row_panel, col_parts, f, after):
    rows, _, width = s.shape
    cols = row_panel.shape[1]
    r = min(STEP_ROWS, rows)
    whole = lambda a: pl.BlockSpec(a.shape, lambda i, p, n=len(a.shape): (0,) * n)
    operands = [s]
    in_specs = [pl.BlockSpec((r, GROUP, width), lambda i, p: (i, chunk, 0))]
    out_shape, out_specs, scratch = [], [], []
    alias = {}
    if back:
        operands.append(row_panel)
        in_specs.append(pl.BlockSpec((r, cols), lambda i, p: (i, 0)))
        b = jax.ShapeDtypeStruct((nq, GROUP // nq, width // nk, cols), F32)
        out_shape += [b] * nk
        out_specs += [whole(b)] * nk
        scratch.append(pltpu.VMEM((GROUP, width, cols), F32))
    if fwd:
        operands += col_parts
        in_specs += [whole(a) for a in col_parts]
        if f is not None:
            alias[len(operands) + 1] = len(out_shape)
            operands.append(f)
            in_specs.append(pl.BlockSpec((r, cols), lambda i, p: (i, 0)))
        out_shape.append(jax.ShapeDtypeStruct((rows, cols), F32))
        out_specs.append(pl.BlockSpec((r, cols), lambda i, p: (i, 0)))
        scratch.append(pltpu.VMEM((GROUP, width, cols), BF16))
    out_shape.append(jax.ShapeDtypeStruct((1, 1), F32))
    out_specs.append(pl.BlockSpec(memory_space=pltpu.SMEM))
    operands += after
    in_specs += [pl.BlockSpec(memory_space=pl.ANY)] * len(after)
    name = "panel_" + ("b" if back else "") + ("f" if fwd else "") + str(chunk)
    out = pl.pallas_call(
        functools.partial(panel_kernel, back, fwd, nk, nq, len(after), f is None, weights),
        grid_spec=pltpu.PrefetchScalarGridSpec(
            num_scalar_prefetch=1,
            grid=(rows // r,),
            in_specs=in_specs,
            out_specs=out_specs,
            scratch_shapes=scratch,
        ),
        out_shape=out_shape,
        input_output_aliases=alias,
        compiler_params=pltpu.CompilerParams(vmem_limit_bytes=VMEM),
        cost_estimate=pl.CostEstimate(
            flops=COST * 2 * rows * GROUP * width * cols * (back + fwd),
            bytes_accessed=2 * rows * GROUP * width,
            transcendentals=0,
        ),
        name=name,
    )(pos, *operands)
    return out[:nk] if back else None, out[-2] if fwd else f, out[-1].reshape(())


def local(trailing_adj, factor_panel, panel_adj, inverse_diag, diag_adjoint):
    row_count, _, block, col_count, _, _ = trailing_adj.shape
    piece, cols = factor_panel.shape[2:]
    nr, nc = lax.axis_size("row"), lax.axis_size("col")
    nq = nr // nc
    order = row_count * nr * block
    scale = 2.0 ** math.floor(math.log2(65504 * 32 / (6 * order)))
    r, c = lax.axis_index("row"), lax.axis_index("col")
    pos = jnp.stack([lax.rem(r, nc), lax.div(r, nc)]).astype(jnp.int32)
    kc = GROUP // nq
    chunks = col_count // GROUP
    s = trailing_adj.reshape(row_count * block, col_count, block)
    mine = factor_panel.reshape(row_count, piece, cols)
    low, high = bits(1, nc), bits(nc, nr)

    def swap(x, bit, axis="row"):
        return lax.ppermute(x, axis, [(i, i ^ bit) for i in range(lax.axis_size(axis))])

    turn = []
    for a in range(nr):
        for b in range(nc):
            turn.append((a * nc + b, ((a // nc) * nc + b) * nc + a % nc))

    def turned(x):
        return lax.ppermute(x, ("row", "col"), turn)

    row_panel = jnp.zeros((row_count, block, cols), BF16)
    for d in range(nc):
        part = mine if d == 0 else swap(mine, d, "col")
        at = jnp.bitwise_xor(c, d) * piece
        row_panel = lax.dynamic_update_slice(row_panel, part, (0, at, 0))
    row_panel = row_panel.reshape(row_count * block, cols)
    own = turned(mine)

    now = None

    def later(x):
        return x if now is None else x + now.astype(x.dtype)

    def gather(p, order):
        got = own[None, p * kc : (p + 1) * kc]
        for bit in order:
            yield [got]
            got = later(jnp.concatenate([got, swap(got, bit)]))
        parts = {0: got}
        for bit in low:
            yield list(parts.values())
            parts.update({d + bit: swap(x, bit) for d, x in parts.items()})
        col_parts[p] = [parts[d] for d in range(nc)]

    def narrow(x):
        return (x * scale).astype(F16)

    def wide(x):
        return x.astype(F32) * (1.0 / scale)

    def reduce(p):
        parts = backs[p]
        for bit in low[::-1]:
            yield []
            parts = [later(x) + swap(y, bit) for x, y in zip(parts[:bit], parts[bit:])]
        total = parts[0]
        half = nq // 2
        kept, message = lax.optimization_barrier((total[:half], narrow(total[half:])))
        yield [kept]
        total = later(kept) + wide(swap(message, nc))
        total, *messages = lax.optimization_barrier(
            (total[0], *[narrow(total[m]) for m in range(1, half)])
        )
        yield [total]
        total = later(total)
        for m, x in enumerate(messages, 1):
            total = total + wide(swap(x, 2 * nc * m))
        sums[p] = total
        yield [total]
        backward[p] = turned(total)

    def step(stream):
        return next(stream, [])

    def finish(stream):
        for _ in stream:
            pass

    y_first = high[:1] + high[:0:-1]
    z_first = high[::-1]
    orders = [z_first if p % 2 else y_first for p in range(chunks)]
    col_parts, backs, sums, backward = ([None] * chunks for _ in range(4))
    gathers = [gather(p, o) for p, o in enumerate(orders)]
    reduces = [reduce(p) for p in range(chunks)]
    slots = [[0, 1, 2, 3], [0, 1, 2, 3], [0, 2, 3, 4], [0, 3, 4, 5]]
    b_weights = [nq // 2] + [1 << i for i in range(len(high) - 1)]
    f = None
    previous = []
    for n in range(2 * chunks):
        after = list(previous)
        for p, stream in enumerate(gathers):
            if n in slots[p % 4]:
                after += step(stream)
        for p, stream in enumerate(reduces):
            if n > p:
                after += step(stream)
        p = n % chunks
        if n < chunks:
            backs[p], _, now = panel_call(
                True, False, p, nc, nq, b_weights, pos, s, row_panel, None, None, after
            )
            previous = [backs[p][0]]
        else:
            finish(gathers[p])
            weights = [0] * len(high)
            for i, bit in enumerate(orders[p]):
                weights[high.index(bit)] = 1 << i
            _, f, now = panel_call(
                False, True, p, nc, nq, weights, pos, s, row_panel, col_parts[p], f, after
            )
            previous = []
    for stream in reduces:
        finish(stream)
    backward = jnp.concatenate(backward)

    split = f.reshape(row_count, nc, piece, cols)
    at = lambda d: lax.dynamic_index_in_dim(split, jnp.bitwise_xor(c, d), 1, keepdims=False)
    forward = at(0)
    for d in range(1, nc):
        forward = forward + wide(swap(narrow(at(d)), d, "col"))
    combined = (panel_adj.reshape(row_count, piece, cols) - forward - backward).reshape(-1, cols)
    panel_grad = jnp.dot(combined, inverse_diag, precision=lax.Precision.HIGHEST)

    tall = (((0,), (0,)), ((), ()))
    exact = lax.Precision.HIGHEST
    flat = lambda x: x.reshape(-1, cols).astype(F32)
    g = lax.dot_general(flat(jnp.concatenate(sums)), flat(own), tall, precision=exact)
    la = lax.dot_general(flat(mine), flat(panel_adj), tall, precision=exact)
    part = la - g - g.T

    def half(x, bit, flip):
        n = x.shape[0] // 2
        which = jnp.bitwise_xor(jnp.bitwise_and(lax.div(r, bit), 1), flip)
        return lax.dynamic_slice_in_dim(x, which * n, n)

    def joined(x, bit):
        got = swap(x, bit)
        first = jnp.bitwise_and(lax.div(r, bit), 1) == 0
        return jnp.concatenate([jnp.where(first, x, got), jnp.where(first, got, x)])

    for bit in (1, 2):
        part = half(part, bit, 0) + swap(half(part, bit, 1), bit)
    part = sum((swap(part, 4 * m) for m in range(1, nr // 4)), part)
    part = sum((swap(part, m, "col") for m in range(1, nc)), part)
    for bit in (2, 1):
        part = joined(part, bit)
    cross = part
    diag_grad = diag_adjoint - jnp.dot(inverse_diag.T, cross.T, precision=lax.Precision.HIGHEST)
    return panel_grad.reshape(factor_panel.shape), diag_grad


def solution(mesh):
    placed = (
        P(None, "row", None, None, "col", None),
        P(None, "row", "col", None),
        P(None, "row", "col", None),
        P(),
        P(),
    )
    return jax.shard_map(
        local,
        mesh=mesh,
        in_specs=placed,
        out_specs=(P(None, "row", "col", None), P()),
        check_vma=False,
    )
```

```python
import functools
import math

import jax
import jax.numpy as jnp
from jax import lax
from jax.experimental import pallas as pl
from jax.experimental.pallas import tpu as pltpu
from jax.sharding import PartitionSpec as P

F32, F16, BF16 = jnp.float32, jnp.float16, jnp.bfloat16
STEP_ROWS = 512
GROUP = 16
VMEM = 56 << 20
COST = 4


def bits(low, high):
    return [1 << i for i in range(low.bit_length() - 1, high.bit_length() - 1)]


def panel_kernel(back, fwd, nk, nq, count, first, many, order, *refs):
    refs = list(refs)
    take = lambda n: [refs.pop(0) for _ in range(n)]
    (pos_ref, s_ref) = take(2)
    (lr_ref,) = take(1) if back else (None,)
    ny = min(2, nq)
    l_refs = take(nk * ny) if fwd else []
    (f_in,) = take(1) if fwd and not first else (None,)
    take(count)
    b_refs = take(many * nk) if back else []
    (f_ref,) = take(1) if fwd else (None,)
    (zero_ref,) = take(1)
    (acc,) = take(1) if back else (None,)
    (col,) = take(1) if fwd else (None,)
    i, c, last = pl.program_id(0), pl.program_id(1), pl.num_programs(0) - 1
    _, group, width = s_ref.shape
    piece = width // nk

    def places():
        for dk in range(nk):
            at = pl.multiple_of(jnp.bitwise_xor(pos_ref[0], dk) * piece, piece)
            for m in range(nq):
                q = jnp.bitwise_xor(pos_ref[1], m)
                for kk in range(group // nq):
                    yield dk, m, kk, kk * nq + q, at

    def part_of(m):
        places = [(m >> bit) & 1 for bit in order]
        return places[-1], sum(p << k for k, p in enumerate(places[:-1]))

    @pl.when(i == 0)
    def _():
        zero_ref[0, 0] = 0.0

    x = jnp.swapaxes(s_ref[...], 0, 1)
    if fwd:

        @pl.when((i == 0) & (c == 0))
        def _():
            for t in range(many):
                for dk, m, kk, j, at in places():
                    part, place = part_of(m)
                    col[t, j, pl.ds(at, piece), :] = l_refs[dk * ny + part][t, place, kk]

        flat = jnp.concatenate([x[j] for j in range(group)], axis=1)
        part = jnp.dot(flat, col[c].reshape(group * width, -1), preferred_element_type=F32)
        if many > 1:

            @pl.when(c == 0)
            def _():
                f_ref[...] = part if first else f_in[...] + part

            @pl.when(c > 0)
            def _():
                f_ref[...] += part

        else:
            f_ref[...] = part if first else f_in[...] + part
    if back:

        def product(j):
            return lax.dot_general(
                x[j], lr_ref[...], (((0,), (0,)), ((), ())), preferred_element_type=F32
            )

        @pl.when(i == 0)
        def _():
            for j in range(group):
                acc[c, j] = product(j)

        @pl.when(i > 0)
        def _():
            for j in range(group):
                acc[c, j] += product(j)

        for t in range(many):

            @pl.when((i == last) & (c == t))
            def _(t=t):
                for dk, m, kk, j, at in places():
                    b_refs[t * nk + dk][m % ny * (nq // ny) + m // ny, kk] = acc[
                        t, j, pl.ds(at, piece), :
                    ]


def panel_call(back, fwd, chunk, many, order, nk, nq, pos, s, row_panel, col_parts, f, after):
    rows, _, width = s.shape
    cols = row_panel.shape[1]
    r = min(STEP_ROWS, rows)
    whole = lambda a: pl.BlockSpec(
        a.shape, lambda i, c, p, n=len(a.shape): (0,) * n, pipeline_mode=pl.Buffered(1)
    )
    operands = [s]
    in_specs = [pl.BlockSpec((r, GROUP, width), lambda i, c, p: (i, chunk + c, 0))]
    out_shape, out_specs, scratch = [], [], []
    alias = {}
    if back:
        operands.append(row_panel)
        in_specs.append(pl.BlockSpec((r, cols), lambda i, c, p: (i, 0)))
        b = jax.ShapeDtypeStruct((nq, GROUP // nq, width // nk, cols), F32)
        out_shape += [b] * (many * nk)
        out_specs += [
            pl.BlockSpec(b.shape, lambda i, c, p, n=len(b.shape): (0,) * n)
        ] * (many * nk)
        scratch.append(pltpu.VMEM((many, GROUP, width, cols), F32))
    if fwd:
        operands += col_parts
        in_specs += [whole(a) for a in col_parts]
        if f is not None:
            alias[len(operands) + 1] = len(out_shape)
            operands.append(f)
            in_specs.append(pl.BlockSpec((r, cols), lambda i, c, p: (i, 0)))
        out_shape.append(jax.ShapeDtypeStruct((rows, cols), F32))
        out_specs.append(pl.BlockSpec((r, cols), lambda i, c, p: (i, 0)))
        scratch.append(pltpu.VMEM((many, GROUP, width, cols), BF16))
    out_shape.append(jax.ShapeDtypeStruct((1, 1), F32))
    out_specs.append(pl.BlockSpec(memory_space=pltpu.SMEM))
    operands += after
    in_specs += [pl.BlockSpec(memory_space=pl.ANY)] * len(after)
    name = "panel_" + ("b" if back else "") + ("f" if fwd else "") + str(chunk)
    out = pl.pallas_call(
        functools.partial(panel_kernel, back, fwd, nk, nq, len(after), f is None, many, order),
        grid_spec=pltpu.PrefetchScalarGridSpec(
            num_scalar_prefetch=1,
            grid=(rows // r, many),
            in_specs=in_specs,
            out_specs=out_specs,
            scratch_shapes=scratch,
        ),
        out_shape=out_shape,
        input_output_aliases=alias,
        compiler_params=pltpu.CompilerParams(vmem_limit_bytes=VMEM),
        cost_estimate=pl.CostEstimate(
            flops=COST * 2 * rows * many * GROUP * width * cols * (back + fwd),
            bytes_accessed=2 * rows * many * GROUP * width,
            transcendentals=0,
        ),
        name=name,
    )(pos, *operands)
    return [out[t * nk : (t + 1) * nk] for t in range(many)] if back else None, out[-2] if fwd else f, out[-1].reshape(())


def join_kernel(*refs):
    refs[-1][0, 0] = 0.0


def join(after):
    out = pl.pallas_call(
        join_kernel,
        in_specs=[pl.BlockSpec(memory_space=pl.ANY)] * len(after),
        out_specs=pl.BlockSpec(memory_space=pltpu.SMEM),
        out_shape=jax.ShapeDtypeStruct((1, 1), F32),
        name="join",
    )(*after)
    return out.reshape(())


def local(trailing_adj, factor_panel, panel_adj, inverse_diag, diag_adjoint):
    row_count, _, block, col_count, _, _ = trailing_adj.shape
    piece, cols = factor_panel.shape[2:]
    nr, nc = lax.axis_size("row"), lax.axis_size("col")
    nq = nr // nc
    order = row_count * nr * block
    scale = 2.0 ** math.floor(math.log2(65504 * 32 / (6 * order)))
    r, c = lax.axis_index("row"), lax.axis_index("col")
    pos = jnp.stack([lax.rem(r, nc), lax.div(r, nc)]).astype(jnp.int32)
    kc = GROUP // nq
    chunks = col_count // GROUP
    s = trailing_adj.reshape(row_count * block, col_count, block)
    mine = factor_panel.reshape(row_count, piece, cols)
    low, high = bits(1, nc), bits(nc, nr)

    def swap(x, bit, axis="row"):
        return lax.ppermute(x, axis, [(i, i ^ bit) for i in range(lax.axis_size(axis))])

    turn = []
    for a in range(nr):
        for b in range(nc):
            turn.append((a * nc + b, ((a // nc) * nc + b) * nc + a % nc))

    def turned(x):
        return lax.ppermute(x, ("row", "col"), turn)

    def narrow(x):
        return (x * scale).astype(F16)

    def wide(x):
        return x.astype(F32) * (1.0 / scale)

    ny = min(2, nq)
    nz = nq // ny
    early = list(range(chunks - 1))
    late = [chunks - 1]
    sets = [x for x in (late, early) if x]
    tokens = []
    own = [turned(mine[x[0] * kc : (x[-1] + 1) * kc]) for x in sets[:1]]
    row_panel = jnp.zeros((row_count, block, cols), BF16)
    for d in range(nc):
        part = mine if d == 0 else swap(mine, d, "col")
        at = jnp.bitwise_xor(c, d) * piece
        row_panel = lax.dynamic_update_slice(row_panel, part, (0, at, 0))
    row_panel = row_panel.reshape(row_count * block, cols)

    own += [turned(mine[x[0] * kc : (x[-1] + 1) * kc]) for x in sets[1:]]

    now = None

    def later(x):
        return x if now is None else x + now.astype(x.dtype)


    around = {}
    col_parts = {}

    def along(i, bit):
        if i not in around:
            around[i] = own[i].reshape(-1, 1, kc, piece, cols)
        x = around[i]
        got = swap(x, bit)
        return lambda: around.update({i: later(jnp.concatenate([x, got], axis=1))})

    def along_last(i, bit, soon):
        x = around[i]
        got = swap(x, bit)
        near = [swap(x, d) for d in range(1, nc)] if soon else None

        def finish():
            far = later(got)
            parts = [x, far]
            for d in range(1, nc):
                parts += [near[d - 1] if soon else swap(x, d), swap(far, d)]
            col_parts[i] = parts

        return finish

    backs = [None] * chunks
    backward = [None] * len(sets)

    def over_kappa(p):
        got = [swap(backs[p][d], d) for d in range(1, nc)]

        def total(cut):
            t = later(backs[p][0][cut])
            for x in got:
                t = t + x[cut]
            return t

        return lambda: (total(slice(0, nz)), total(slice(nz, None)) if ny > 1 else None)

    def over_y(pairs):
        tokens.extend(kept for kept, _ in pairs)
        if ny == 1:
            return lambda: [later(kept) for kept, _ in pairs]
        got = swap(narrow(jnp.stack([other for _, other in pairs])), nc)
        return lambda: [later(kept) + wide(got[t]) for t, (kept, _) in enumerate(pairs)]

    def over_z(totals):
        part = lambda m: jnp.concatenate([t[m] for t in totals])
        first = part(0)
        tokens.append(first)
        got = [swap(narrow(part(m)), ny * nc * m) for m in range(1, nz)]
        return lambda: sum((wide(x) for x in got), later(first))

    f = None

    def call(back, fwd, p, many=1):
        nonlocal f, now
        i = 0 if p in sets[0] else 1
        parts = col_parts[i] if fwd else None
        after = tokens + last
        got, f, now = panel_call(
            back, fwd, p, many, orders[i], nc, nq, pos, s, row_panel, parts, f, after
        )
        tokens.clear()
        last.clear()
        if back:
            backs[p : p + many] = got
            if not fwd:
                last.append(got[0][0])

    last = []
    orders = [tuple(range(len(high)))[::-1], (0, *range(len(high) - 1, 0, -1))]
    links = [[nc << bit for bit in order] for order in orders]
    if early:
        z1, z0, y = links[0]
        along(0, z1)()
        got_l = along(0, z0)
        got_e = along(1, y)
        tokens.append(around[0])
        call(True, False, 0)
        got_l()
        got_e()
        got_e = along(1, z1)
        got_l = along_last(0, y, True)
        core0 = over_kappa(0)
        tokens += [around[0], around[1]]
        call(True, False, 1)
        core1 = over_kappa(1)
        got_l()
        y0 = over_y([core0()])
        tokens += col_parts[0][1:2]
        call(True, False, 2)
        core2 = over_kappa(2)
        got_e()
        got_e = along_last(1, z0, True)
        (t0,) = y0()
        y1 = over_y([core1()])
        tokens += [t0, around[1]]
        call(True, True, 3)
        core3 = over_kappa(3)
        got_e()
        (t1,) = y1()
        z01 = over_z([t0, t1])
        y23 = over_y([core2(), core3()])
        call(False, True, 0, 3)
        first = z01()
        backward[0] = turned(first)
        t2, t3 = y23()
        now = join([first, t2, t3, f])
        f = later(f)
        pending = [t2, t3]
    else:
        for bit in links[0][:-1]:
            along(0, bit)()
        along_last(0, links[0][-1], False)()
        call(True, True, 0)
        pending = over_y([over_kappa(p)() for p in late])()
    split = f.reshape(row_count, nc, piece, cols)
    at = lambda d: lax.dynamic_index_in_dim(split, jnp.bitwise_xor(c, d), 1, keepdims=False)
    forward = at(0)
    for d in range(1, nc):
        forward = forward + wide(swap(narrow(at(d)), d, "col"))
    total = jnp.concatenate(pending, axis=1)
    for bit in high[1:]:
        n = total.shape[0] // 2
        total = total.reshape(n, 2, *total.shape[1:])
        total = total[:, 0] + wide(swap(narrow(total[:, 1]), bit))
        if bit == high[1]:
            now = join([total, forward])
    backward[-1] = turned(total[0])
    backward = jnp.concatenate(backward)

    combined = (panel_adj.reshape(row_count, piece, cols) - forward - backward).reshape(-1, cols)
    panel_grad = jnp.dot(combined, inverse_diag, precision=lax.Precision.HIGHEST)

    tall = (((0,), (0,)), ((), ()))
    exact = lax.Precision.HIGHEST
    flat = lambda x: x.reshape(-1, cols).astype(F32)
    g = lax.dot_general(flat(row_panel), f, tall, precision=exact)
    la = lax.dot_general(flat(mine), flat(panel_adj), tall, precision=exact)
    part = later(la - g - g.T)

    def half(x, bit, flip):
        n = x.shape[0] // 2
        which = jnp.bitwise_xor(jnp.bitwise_and(lax.div(r, bit), 1), flip)
        return lax.dynamic_slice_in_dim(x, which * n, n)

    def joined(x, bit):
        got = swap(x, bit)
        first = jnp.bitwise_and(lax.div(r, bit), 1) == 0
        return jnp.concatenate([jnp.where(first, x, got), jnp.where(first, got, x)])

    for bit in (1, 2):
        part = half(part, bit, 0) + swap(half(part, bit, 1), bit)
    for bit in bits(4, nr):
        part = part + swap(part, bit)
    part = sum((swap(part, m, "col") for m in range(1, nc)), part)
    for bit in (2, 1):
        part = joined(part, bit)
    cross = part
    diag_grad = diag_adjoint - jnp.dot(inverse_diag.T, cross.T, precision=lax.Precision.HIGHEST)
    return panel_grad.reshape(factor_panel.shape), diag_grad


def solution(mesh):
    placed = (
        P(None, "row", None, None, "col", None),
        P(None, "row", "col", None),
        P(None, "row", "col", None),
        P(),
        P(),
    )
    return jax.shard_map(
        local,
        mesh=mesh,
        in_specs=placed,
        out_specs=(P(None, "row", "col", None), P()),
        check_vma=False,
    )
```
